512 devices in a mesh: section: 4 (over x), ctx: 64 (over z, y_lo, core), tp: 2 (over y_hi).
Axes of the slice: x: 4, y: 8 (y_hi: 2, y_lo: 4; y = y_hi * 4 + y_lo), z: 8, core: 2. Of those that a mesh axis runs over, the one named last changes fastest.
Arguments:
- teacher_hidden: bfloat16 [1024, 16384], P('ctx', ('section', 'tp')), may hold values from -21 to 21
- lm_head: bfloat16 [16384, 65536], P(('section', 'tp'), 'ctx'), may hold values from -2.5 to 2.5
- sampled_ids: int32 [1024], replicated, may hold values from 0 to 65535
- student_logprob: float32 [1024], replicated, may hold values from -24 to -4
- owner_map: int32 [1024], replicated, may hold values from 0 to 8191
- queries: bfloat16 [8192, 8192], P('ctx', ('section', 'tp')), may hold values from -108 to 108
- keys: bfloat16 [8192, 1024], P('ctx', ('section', 'tp')), may hold values from -6 to 6
- values: bfloat16 [8192, 1024], P('ctx', ('section', 'tp')), may hold values from -6 to 6
- grad_out: bfloat16 [8192, 8192], P('ctx', ('section', 'tp')), may hold values from -24 to 24
- segment_ids: int32 [8192], P('ctx'), may hold values from 0 to 15, never falling along the last dimension, each value on 1 to 1025 neighbouring positions
Outputs:
- advantage: float32 [1024], P(('section', 'tp'))
- d_queries: bfloat16 [8192, 8192], P('ctx', ('section', 'tp'))
- d_keys: bfloat16 [8192, 1024], P('ctx', ('section', 'tp'))
- d_values: bfloat16 [8192, 1024], P('ctx', ('section', 'tp'))
The draws below stay inside these ranges and needn't reach their ends.
Inputs may be any that keep to these rules, and one draw needn't show every extreme that they name: `segment_ids`: segment numbers never fall along the sequence; a segment holds 1 to 1025 positions and one holds exactly 1025.
All inputs are finite; a program needn't handle non-finite values.
Results may differ from the reference program's by a relative error of at most 0.008.
Values may be sent and summed in bfloat16 or wider, within the bound.
No kernel may reach another device: no remote copies, remote signals or barrier semaphores. Data moves between devices by JAX's collectives and lax.ppermute only.
A program may use at most 128 MiB of HBM per device.

```python
import math
import jax
import jax.numpy as jnp
import numpy as np
from jax import lax

DT = 16384
VOCAB = 65536
TT = 1024
QUERY_HEADS = 64
KEY_VALUE_HEADS = 8
HEAD_SIZE = 128
S_DEV = 128
PACKED_TOKENS = 8192
REACH = 8
DOC_MAX = 1025
SEGS = 16
N_CTX = 64


def shared_direction(key):
    inner_product = jax.random.fold_in(key, 101)
    return jnp.clip(jax.random.normal(inner_product, (DT,), jnp.float32), -6.0, 6.0)


def shared_keys(key):
    inner_product = jax.random.fold_in(key, 202)
    return jnp.clip(jax.random.normal(inner_product, (PACKED_TOKENS, KEY_VALUE_HEADS * HEAD_SIZE), jnp.float32), -6.0, 6.0)


def draw_lm_head(key, part):
    direction = shared_direction(key)
    key = jax.random.fold_in(key, 1)
    noise_key, factor_key = jax.random.split(key)
    noise = jnp.clip(jax.random.normal(noise_key, (DT, VOCAB), jnp.float32), -6.0, 6.0)
    columns = jnp.arange(VOCAB, dtype=jnp.int32)
    rising = jnp.exp(math.log(10.0) * columns.astype(jnp.float32) / VOCAB)
    factor = jnp.exp(math.log(2.0) * jax.random.uniform(factor_key, (VOCAB,), jnp.float32))
    column_scale = 0.15 * rising * factor
    matrix = noise * column_scale[None, :] * DT ** (-0.5)
    first_special = VOCAB // 3
    special = direction[:, None] * DT ** (-0.5) * jnp.where(columns == first_special, 1.0, 0.994)[None, :]
    chosen = (columns == first_special) | (columns == first_special + 1)
    matrix = jnp.where(chosen[None, :], special, matrix)
    return jnp.clip(matrix, -2.5, 2.5).astype(jnp.bfloat16)


def draw_teacher_hidden(key, part):
    key = jax.random.fold_in(key, 2)
    hidden = jnp.clip(jax.random.normal(key, (TT, DT), jnp.float32), -6.0, 6.0)
    return hidden.astype(jnp.bfloat16)


def draw_keys(key, part):
    base_vectors = shared_keys(key)
    return base_vectors.astype(jnp.bfloat16)


def draw_queries(key, part):
    key = jax.random.fold_in(key, 3)
    noise = jnp.clip(jax.random.normal(key, (PACKED_TOKENS, QUERY_HEADS * HEAD_SIZE), jnp.float32), -6.0, 6.0)
    return noise.astype(jnp.bfloat16)


def place_ends(drawn, rng, smallest, top_value):
    extent = drawn.shape
    spot = [jax.random.randint(jax.random.fold_in(rng, axis), (), 0, extent[axis]) for axis in range(len(extent))]
    drawn = drawn.at[tuple(spot)].set(smallest)
    longest = extent.index(max(extent))
    spot[longest] = (spot[longest] + 1) % extent[longest]
    return drawn.at[tuple(spot)].set(top_value)


def block_levels(rng, extent, cuts, least, top_value):
    factor_of, own = 1.0, jax.random.fold_in(rng, 6)
    for dim, blocks in cuts:
        steps = jnp.exp(jax.random.uniform(jax.random.fold_in(own, dim), (blocks,), jnp.float32, least / len(cuts), top_value / len(cuts)))
        factor_of = factor_of * jnp.repeat(steps, extent[dim] // blocks).reshape([-1 if axis == dim else 1 for axis in range(len(extent))])
    return factor_of


def rank_table(number_of, lean):
    loads = [(1 << 20) // math.isqrt(rank ** lean) + 1 for rank in range(1, number_of + 1)]
    deviation = 1 + sum(loads) // (1 << 30)
    return np.cumsum(np.array([max(1, weight // deviation) for weight in loads]))


def ranked(key, shape, count, slope):
    table = rank_table(count, slope)
    pick = jax.random.randint(jax.random.fold_in(key, 1), shape, 0, int(table[count - 1]))
    standing = jnp.searchsorted(jnp.asarray(table, jnp.int32), pick, side="right")
    return jax.random.permutation(jax.random.fold_in(key, 2), count)[standing].astype(jnp.int32)


def length_profile(count, total, reach, skew):
    loads = [(1 << 20) // math.isqrt(rank ** skew) + 1 for rank in range(2, count + 1)]
    rest, counts = total - reach - (count - 1), [1] * (count - 1)
    while rest > 0:
        candidates = [i for i in range(count - 1) if counts[i] < reach]
        mass, budget = sum([loads[i] for i in candidates]), rest
        for i in candidates:
            addition = min(reach - counts[i], max(1, budget * loads[i] // mass), rest)
            counts[i] = counts[i] + addition
            rest = rest - addition
    return np.array([reach] + counts)


def uneven(own_key, number_of, total, reach, skew):
    if number_of == 2:
        one = jax.random.randint(own_key, (), max(1, total - reach), min(reach, total - 1) + 1)
        return jnp.stack([one, total - one])
    lengths = jnp.asarray(length_profile(number_of, total, reach, skew), jnp.int32)
    twos = (number_of - 1) // 2
    donor, taker = lengths[1:1 + 2 * twos:2], lengths[2:2 + 2 * twos:2]
    slack = jnp.minimum(donor - 1, reach - taker)
    moved = jax.random.randint(jax.random.fold_in(own_key, 1), (twos,), 0, 1 << 20) % (slack + 1)
    lengths = lengths.at[1:1 + 2 * twos:2].set(donor - moved).at[2:2 + 2 * twos:2].set(taker + moved)
    return lengths[jax.random.permutation(jax.random.fold_in(own_key, 2), number_of)]


def bell_draw(rng, shape, width, reach, shards=(), kind=jnp.bfloat16):
    gain = block_levels(rng, shape, shards, -0.22, 0.18) if shards else 1.0
    result = jax.random.normal(rng, shape, jnp.float32) * width * gain
    return jnp.minimum(jnp.maximum(result, -reach), reach).astype(kind)


def setup_inputs(seed: int = 0) -> dict:
    arg_keys = jax.random.split(jax.random.key(seed), 11)
    teacher_hidden = draw_teacher_hidden(jax.random.fold_in(arg_keys[10], 71), 0)
    lm_head = draw_lm_head(jax.random.fold_in(arg_keys[10], 71), 0)
    sampled_ids = place_ends(ranked(arg_keys[2], (TT,), VOCAB, 2), jax.random.fold_in(arg_keys[2], 3), 0, VOCAB - 1).astype(jnp.int32)
    student_logprob = jnp.clip(jax.random.uniform(arg_keys[3], (TT,), jnp.float32, -24.0, -4.0), -24.0, -4.0)
    owner_map = place_ends(jax.random.randint(arg_keys[4], (TT,), 0, PACKED_TOKENS), jax.random.fold_in(arg_keys[4], 1), 0, PACKED_TOKENS - 1).astype(jnp.int32)
    queries = draw_queries(jax.random.fold_in(arg_keys[10], 71), 0)
    keys = draw_keys(jax.random.fold_in(arg_keys[10], 71), 0)
    values = bell_draw(arg_keys[7], (PACKED_TOKENS, KEY_VALUE_HEADS * HEAD_SIZE), 1.0, 6.0, ((0, 64), (1, 8)))
    grad_out = bell_draw(arg_keys[8], (PACKED_TOKENS, QUERY_HEADS * HEAD_SIZE), 4.0, 24.0, ((0, 64), (1, 8)))
    segment_ids = jnp.searchsorted(jnp.cumsum(uneven(arg_keys[9], SEGS, PACKED_TOKENS, DOC_MAX, 2)), jnp.arange(PACKED_TOKENS), side="right").astype(jnp.int32)
    return {"teacher_hidden": teacher_hidden, "lm_head": lm_head, "sampled_ids": sampled_ids, "student_logprob": student_logprob, "owner_map": owner_map, "queries": queries, "keys": keys, "values": values, "grad_out": grad_out, "segment_ids": segment_ids}


advantage_scale = 0.1
clip_bound = 8.0
masked_value = -1.0e30


def normalize(scores, allowed):
    masked = jnp.where(allowed, scores, masked_value)
    row_top = jnp.max(masked, axis=1, keepdims=True)
    row_total = jnp.sum(jnp.where(allowed, jnp.exp(masked - row_top), 0.0), axis=1, keepdims=True)
    log_norm = row_top + jnp.log(row_total)
    return jnp.where(allowed, jnp.exp(masked - log_norm), 0.0).astype(jnp.bfloat16)


def attend_block(query_rows, upstream, key_window, value_window, allowed, scaling):
    scores = jnp.dot(query_rows, key_window.T, preferred_element_type=jnp.float32) * scaling
    softmax = normalize(scores, allowed)
    context = jnp.dot(softmax, value_window, preferred_element_type=jnp.float32)
    row_delta = jnp.sum(upstream.astype(jnp.float32) * context, axis=1, keepdims=True)
    grad_prob = jnp.dot(upstream, value_window.T, preferred_element_type=jnp.float32)
    grad_score = (softmax.astype(jnp.float32) * (grad_prob - row_delta) * scaling).astype(jnp.bfloat16)
    grad_query = jnp.dot(grad_score, key_window, preferred_element_type=jnp.float32)
    grad_key = jnp.dot(grad_score.T, query_rows, preferred_element_type=jnp.float32)
    grad_value = jnp.dot(softmax.T, upstream, preferred_element_type=jnp.float32)
    return grad_query, grad_key, grad_value


def reference(teacher_hidden, lm_head, sampled_ids, student_logprob, owner_map, queries, keys, values, grad_out, segment_ids):
    logits = jnp.dot(teacher_hidden, lm_head, preferred_element_type=jnp.float32)
    row_top = jnp.max(logits, axis=1)
    row_total = jnp.sum(jnp.exp(logits - row_top[:, None]), axis=1)
    picked = jnp.take_along_axis(logits, sampled_ids[:, None], axis=1)[:, 0]
    teacher_logprob = picked - row_top - jnp.log(row_total)
    advantage = jnp.clip(teacher_logprob - student_logprob, -clip_bound, clip_bound)
    routed = jax.ops.segment_sum(advantage, owner_map, num_segments=PACKED_TOKENS)
    weight = 1.0 + advantage_scale * routed
    upstream = (weight[:, None] * grad_out.astype(jnp.float32)).astype(jnp.bfloat16)
    queries_per_group = QUERY_HEADS // KEY_VALUE_HEADS
    padding = REACH * S_DEV
    window_size = padding + S_DEV
    scaling = HEAD_SIZE ** -0.5
    positions = jnp.arange(PACKED_TOKENS + padding, dtype=jnp.int32) - padding
    segments_padded = jnp.concatenate([jnp.zeros((padding,), jnp.int32), segment_ids])
    offsets = jnp.arange(S_DEV, dtype=jnp.int32)
    query_pieces = []
    key_pieces = []
    value_pieces = []
    for head_group_index in range(KEY_VALUE_HEADS):
        query_group = queries[:, head_group_index * queries_per_group * HEAD_SIZE:(head_group_index + 1) * queries_per_group * HEAD_SIZE]
        upstream_group = upstream[:, head_group_index * queries_per_group * HEAD_SIZE:(head_group_index + 1) * queries_per_group * HEAD_SIZE]
        keys_padded = jnp.concatenate([jnp.zeros((padding, HEAD_SIZE), jnp.bfloat16), keys[:, head_group_index * HEAD_SIZE:(head_group_index + 1) * HEAD_SIZE]])
        values_padded = jnp.concatenate([jnp.zeros((padding, HEAD_SIZE), jnp.bfloat16), values[:, head_group_index * HEAD_SIZE:(head_group_index + 1) * HEAD_SIZE]])

        def advance(carried, block_index):
            key_grads, value_grads = carried
            first_row = block_index * S_DEV
            query_block = lax.dynamic_slice_in_dim(query_group, first_row, S_DEV, 0)
            upstream_block = lax.dynamic_slice_in_dim(upstream_group, first_row, S_DEV, 0)
            query_rows = query_block.reshape(S_DEV, queries_per_group, HEAD_SIZE).transpose(1, 0, 2).reshape(queries_per_group * S_DEV, HEAD_SIZE)
            upstream_rows = upstream_block.reshape(S_DEV, queries_per_group, HEAD_SIZE).transpose(1, 0, 2).reshape(queries_per_group * S_DEV, HEAD_SIZE)
            key_window = lax.dynamic_slice_in_dim(keys_padded, first_row, window_size, 0)
            value_window = lax.dynamic_slice_in_dim(values_padded, first_row, window_size, 0)
            key_position = lax.dynamic_slice_in_dim(positions, first_row, window_size, 0)
            key_segment = lax.dynamic_slice_in_dim(segments_padded, first_row, window_size, 0)
            query_position = first_row + offsets
            query_segment = lax.dynamic_slice_in_dim(segment_ids, first_row, S_DEV, 0)
            doc_mask = (key_segment[None, :] == query_segment[:, None]) & (key_position[None, :] <= query_position[:, None]) & (key_position[None, :] >= 0)
            grad_query, grad_key, grad_value = attend_block(query_rows, upstream_rows, key_window, value_window, jnp.tile(doc_mask, (queries_per_group, 1)), scaling)
            key_grads = lax.dynamic_update_slice_in_dim(key_grads, lax.dynamic_slice_in_dim(key_grads, first_row, window_size, 0) + grad_key, first_row, 0)
            value_grads = lax.dynamic_update_slice_in_dim(value_grads, lax.dynamic_slice_in_dim(value_grads, first_row, window_size, 0) + grad_value, first_row, 0)
            query_grad = grad_query.astype(jnp.bfloat16).reshape(queries_per_group, S_DEV, HEAD_SIZE).transpose(1, 0, 2).reshape(S_DEV, queries_per_group * HEAD_SIZE)
            return (key_grads, value_grads), query_grad

        initial = (jnp.zeros((PACKED_TOKENS + padding, HEAD_SIZE), jnp.float32), jnp.zeros((PACKED_TOKENS + padding, HEAD_SIZE), jnp.float32))
        (key_grads, value_grads), query_blocks = lax.scan(advance, initial, jnp.arange(N_CTX, dtype=jnp.int32))
        query_pieces.append(query_blocks.reshape(PACKED_TOKENS, queries_per_group * HEAD_SIZE))
        key_pieces.append(key_grads[padding:].astype(jnp.bfloat16))
        value_pieces.append(value_grads[padding:].astype(jnp.bfloat16))
    d_queries = jnp.concatenate(query_pieces, axis=1)
    d_keys = jnp.concatenate(key_pieces, axis=1)
    d_values = jnp.concatenate(value_pieces, axis=1)
    return (advantage, d_queries, d_keys, d_values)
```

```python
import jax
import jax.numpy as jnp
from jax import lax
from jax.sharding import PartitionSpec as P

advantage_scale = 0.1
clip_bound = 8.0
masked_value = -1e30

Z, Y, CORES = 8, 4, 2
SECTIONS, TPS = 4, 2
PIECE = 16
FARTHEST = 8


def ctx_move(block, target):
    route = []
    for z in range(Z):
        for y in range(Y):
            for core in range(CORES):
                z2, y2, core2 = target(z, y, core)
                route.append(
                    (z * 8 + y * 2 + core, (z2 % Z) * 8 + (y2 % Y) * 2 + core2 % CORES)
                )
    return lax.ppermute(block, "ctx", route)


def over_y(block, bits):
    return ctx_move(block, lambda z, y, core: (z, y ^ bits, core))


def along_all_z(block):
    groups = [[z * 8 + rest for z in range(Z)] for rest in range(Y * CORES)]
    return lax.all_gather(block, "ctx", axis_index_groups=groups)


def other_core(block):
    return ctx_move(block, lambda z, y, core: (z, y, core + 1))


def passed_along(block, distance):
    count = Z * Y * CORES
    route = [(i - distance, i) for i in range(count) if 0 <= i - distance < count]
    return lax.ppermute(block, "ctx", route)


def along_section(block, step):
    return lax.ppermute(block, "section", [(s, (s + step) % SECTIONS) for s in range(SECTIONS)])


def to_other_tp(block):
    return lax.ppermute(block, "tp", [(0, 1), (1, 0)])


def section_parts(gathered, heads, section):
    rows = gathered.shape[1]
    parts = []
    for head in heads:
        part = jnp.dot(
            gathered.reshape(Z * rows, -1), head, preferred_element_type=jnp.float32
        )
        parts.append(part.reshape(SECTIONS, 2, rows // PIECE, PIECE, head.shape[1]))

    def rows_for(step):
        place = lax.rem(section + step, SECTIONS)
        return jnp.stack(
            [lax.dynamic_index_in_dim(part, place, 0, keepdims=False) for part in parts]
        )

    return [rows_for(0)] + [rows_for(step).astype(jnp.bfloat16) for step in (1, 2, 3)]


def section_sums(parts):
    total = parts[0]
    for step in (1, 2, 3):
        total = total + along_section(parts[step], step).astype(jnp.float32)
    return total


def tp_halves(total, tp):
    halves = total.reshape(total.shape[:3] + (TPS, PIECE // TPS) + total.shape[4:])
    keep = lax.dynamic_index_in_dim(halves, tp, 3, keepdims=False)
    give = lax.dynamic_index_in_dim(halves, 1 - tp, 3, keepdims=False)
    return keep, give.astype(jnp.bfloat16)


def tp_sums(keep, give):
    return keep + to_other_tp(give).astype(jnp.float32)


def row_stats(logits, columns, ids):
    picked = jnp.sum(jnp.where(columns == ids[None, ..., None], logits, 0.0), axis=(0, 4))
    row_top = jnp.max(logits, axis=(0, 4))
    row_total = jnp.sum(jnp.exp(logits - row_top[None, ..., None]), axis=(0, 4))
    return jnp.stack([row_top, row_total, picked])


def y_exchanged(array, axis, y):
    shape = array.shape
    pairs = array.reshape(shape[:axis] + (2, 2) + shape[axis + 1 :])
    pairs = jnp.where(y % 2 == 1, jnp.flip(pairs, axis + 1), pairs)
    pairs = jnp.where(y // 2 == 1, jnp.flip(pairs, axis), pairs)
    return pairs.reshape(shape)


def key_value_window(keys, values, segment_ids):
    id_row = jnp.concatenate([segment_ids, jnp.zeros_like(segment_ids)])[None, :]
    own = jnp.concatenate(
        [
            jnp.concatenate([keys, values], axis=1),
            jnp.broadcast_to(id_row.astype(jnp.bfloat16), (16, 2 * keys.shape[1])),
        ],
        axis=0,
    )[None]
    two = jnp.concatenate([passed_along(own, 1), own], axis=0)
    four = jnp.concatenate([passed_along(two, 2), two], axis=0)
    return jnp.concatenate([passed_along(own, 8), passed_along(four, 4), four], axis=0)


def body(
    teacher_hidden,
    lm_head,
    sampled_ids,
    student_logprob,
    owner_map,
    queries,
    keys,
    values,
    grad_out,
    segment_ids,
):
    ctx_index = lax.axis_index("ctx")
    section = lax.axis_index("section")
    tp = lax.axis_index("tp")
    y, core = lax.rem(ctx_index // 2, 4), lax.rem(ctx_index, 2)

    near = jnp.concatenate([teacher_hidden, over_y(teacher_hidden, 1)], axis=0)
    far = over_y(near, 2)
    far, segment_ids = lax.optimization_barrier((far, segment_ids))
    window = key_value_window(keys, values, segment_ids)
    near_all, far, other_head, window = lax.optimization_barrier(
        (along_all_z(near), far, other_core(lm_head), window)
    )
    far_all = along_all_z(far)
    heads = (lm_head, other_head)
    keep, give = tp_halves(section_sums(section_parts(near_all, heads, section)), tp)
    give, far_all, window = lax.optimization_barrier((give, far_all, window))
    near_logits = tp_sums(keep, give)
    far_parts = section_parts(far_all, heads, section)
    far_logits = tp_sums(*tp_halves(section_sums(far_parts), tp))

    def kept(array, axis):
        return lax.dynamic_index_in_dim(
            lax.dynamic_index_in_dim(array, section, 0, keepdims=False), tp, axis, keepdims=False
        )

    token_ids = kept(sampled_ids.reshape(SECTIONS, 2, Y, CORES, TPS, PIECE // TPS), 3)
    token_ids = lax.dynamic_index_in_dim(token_ids, core, 2, keepdims=False)
    relative_ids = y_exchanged(token_ids, 1, y)
    vocab = lm_head.shape[1]
    starts = jnp.stack([ctx_index, ctx_index + 1 - 2 * core]) * vocab
    columns = starts[:, None, None, None, None] + jnp.arange(vocab, dtype=jnp.int32)
    stats = jnp.concatenate(
        [
            row_stats(near_logits, columns, relative_ids[:, :2]),
            row_stats(far_logits, columns, relative_ids[:, 2:]),
        ],
        axis=2,
    )
    stats = y_exchanged(stats, 2, y).reshape(3, -1)
    everywhere = lax.all_to_all(
        jnp.broadcast_to(stats, (Z * Y * CORES,) + stats.shape), "ctx", 0, 0
    ).reshape(Z * Y, CORES, 3, -1)
    highest = jnp.max(everywhere[:, :, 0], axis=0)
    summed = jnp.sum(everywhere[:, :, 1] * jnp.exp(everywhere[:, :, 0] - highest), axis=0)
    teacher_logprob = jnp.sum(everywhere[:, :, 2], axis=0) - highest - jnp.log(summed)
    student_rows = kept(student_logprob.reshape(SECTIONS, 2, Y, CORES, TPS, PIECE // TPS), 3)
    student_rows = student_rows.transpose(2, 0, 1, 3).reshape(CORES, -1)
    advantage = jnp.clip(teacher_logprob - student_rows, -clip_bound, clip_bound).reshape(-1)
    count = SECTIONS * TPS
    everything = lax.all_to_all(
        jnp.broadcast_to(advantage, (count,) + advantage.shape), ("section", "tp"), 0, 0
    )
    owners = owner_map.reshape(SECTIONS, 2, Y, CORES, TPS, PIECE // TPS)
    owners = owners.transpose(0, 4, 3, 1, 2, 5).reshape(-1)
    advantage_own = everything.reshape(SECTIONS, TPS, CORES, 2, Y, PIECE // TPS)
    advantage_own = kept(advantage_own, 2).transpose(2, 1, 0, 3).reshape(-1)
    everything = everything.reshape(-1)

    seq_rows = queries.shape[0]
    head_dim = keys.shape[1]
    group = queries.shape[1] // head_dim
    scaling = head_dim ** (-0.5)
    query_position = ctx_index * seq_rows + jnp.arange(seq_rows, dtype=jnp.int32)
    routed = jnp.sum(
        jnp.where(owners[None, :] == query_position[:, None], everything[None, :], 0.0), axis=1
    )
    weight = 1.0 + advantage_scale * routed

    key_window = window[:, :seq_rows, :head_dim].reshape(-1, head_dim)
    value_window = window[:, :seq_rows, head_dim:].reshape(-1, head_dim)
    key_segment = window[:, seq_rows, :seq_rows].reshape(-1)
    key_position = (ctx_index - FARTHEST) * seq_rows + jnp.arange(
        (FARTHEST + 1) * seq_rows, dtype=jnp.int32
    )
    allowed = (
        (key_segment[None, :] == segment_ids.astype(jnp.bfloat16)[:, None])
        & (key_position[None, :] <= query_position[:, None])
        & (key_position[None, :] >= 0)
    )
    allowed = jnp.tile(allowed, (group, 1))

    def by_head(array):
        return (
            array.reshape(seq_rows, group, head_dim)
            .transpose(1, 0, 2)
            .reshape(group * seq_rows, head_dim)
        )

    query_rows, grad_rows = by_head(queries), by_head(grad_out)
    scores = jnp.dot(query_rows, key_window.T, preferred_element_type=jnp.float32) * scaling
    masked = jnp.where(allowed, scores, masked_value)
    top = jnp.max(masked, axis=1, keepdims=True)
    raised = jnp.where(allowed, jnp.exp(masked - top), 0.0)
    softmax = (raised / jnp.sum(raised, axis=1, keepdims=True)).astype(jnp.bfloat16)
    context = jnp.dot(softmax, value_window, preferred_element_type=jnp.float32)
    row_delta = jnp.sum(grad_rows.astype(jnp.float32) * context, axis=1, keepdims=True)
    grad_prob = jnp.dot(grad_rows, value_window.T, preferred_element_type=jnp.float32)
    grad_score = (softmax.astype(jnp.float32) * (grad_prob - row_delta) * scaling).astype(
        jnp.bfloat16
    )
    grad_query = jnp.dot(grad_score, key_window, preferred_element_type=jnp.float32)

    row_weight = jnp.tile(weight, (group,))[:, None]
    grad_query = (row_weight * grad_query).astype(jnp.bfloat16)
    weighted_query = (row_weight * query_rows.astype(jnp.float32)).astype(jnp.bfloat16)
    weighted_grad = (row_weight * grad_rows.astype(jnp.float32)).astype(jnp.bfloat16)
    grad_key = jnp.dot(grad_score.T, weighted_query, preferred_element_type=jnp.float32)
    grad_value = jnp.dot(softmax.T, weighted_grad, preferred_element_type=jnp.float32)
    both = jnp.concatenate([grad_key, grad_value], axis=1).reshape(
        FARTHEST + 1, seq_rows, 2 * head_dim
    )
    total = both[FARTHEST]
    for distance in range(1, FARTHEST + 1):
        given = both[FARTHEST - distance].astype(jnp.bfloat16)
        total = total + passed_along(given, -distance).astype(jnp.float32)
    total = total.astype(jnp.bfloat16)
    d_queries = (
        grad_query.reshape(group, seq_rows, head_dim)
        .transpose(1, 0, 2)
        .reshape(seq_rows, group * head_dim)
    )
    return (advantage_own, d_queries, total[:, :head_dim], total[:, head_dim:])


def solution(mesh):
    in_specs = (
        P("ctx", ("section", "tp")),
        P(("section", "tp"), "ctx"),
        P(),
        P(),
        P(),
        P("ctx", ("section", "tp")),
        P("ctx", ("section", "tp")),
        P("ctx", ("section", "tp")),
        P("ctx", ("section", "tp")),
        P("ctx"),
    )
    out_specs = (
        P(("section", "tp")),
        P("ctx", ("section", "tp")),
        P("ctx", ("section", "tp")),
        P("ctx", ("section", "tp")),
    )
    return jax.shard_map(body, mesh=mesh, in_specs=in_specs, out_specs=out_specs, check_vma=False)
```

```python
import jax
import jax.numpy as jnp
from jax import lax
from jax.sharding import PartitionSpec as P

advantage_scale = 0.1
clip_bound = 8.0
masked_value = -1e30

Z, Y, CORES = 8, 4, 2
SECTIONS, TPS = 4, 2
PIECE = 16
FARTHEST = 8


def ctx_move(block, target):
    route = []
    for z in range(Z):
        for y in range(Y):
            for core in range(CORES):
                z2, y2, core2 = target(z, y, core)
                route.append(
                    (z * 8 + y * 2 + core, (z2 % Z) * 8 + (y2 % Y) * 2 + core2 % CORES)
                )
    return lax.ppermute(block, "ctx", route)


def across_chips(block):
    groups = [[chip * CORES + core for chip in range(Z * Y)] for core in range(CORES)]
    copies = jnp.broadcast_to(block, (Z * Y,) + block.shape)
    return lax.all_to_all(copies, "ctx", 0, 0, axis_index_groups=groups)


def across_row(blocks):
    row = Y * CORES
    groups = [[z * row + place for place in range(row)] for z in range(Z)]
    return lax.all_to_all(blocks, "ctx", 0, 0, axis_index_groups=groups)


def other_core(block):
    return ctx_move(block, lambda z, y, core: (z, y, core + 1))


def passed_along(block, distance):
    count = Z * Y * CORES
    route = [(i - distance, i) for i in range(count) if 0 <= i - distance < count]
    return lax.ppermute(block, "ctx", route)


def along_section(block, step):
    return lax.ppermute(block, "section", [(s, (s + step) % SECTIONS) for s in range(SECTIONS)])


def to_other_tp(block):
    return lax.ppermute(block, "tp", [(0, 1), (1, 0)])


def section_parts(gathered, weight, section):
    mine = gathered.reshape(-1, gathered.shape[2])
    parts = []
    for rows in (mine, other_core(mine)):
        part = jnp.dot(rows, weight, preferred_element_type=jnp.float32)
        parts.append(part.reshape(SECTIONS, 2, Y, PIECE, weight.shape[1]))

    def rows_for(step):
        place = lax.rem(section + step, SECTIONS)
        return jnp.stack(
            [lax.dynamic_index_in_dim(part, place, 0, keepdims=False) for part in parts]
        )

    return [rows_for(0)] + [rows_for(step).astype(jnp.bfloat16) for step in (1, 2, 3)]


def section_sums(parts):
    total = parts[0]
    for step in (1, 2, 3):
        total = total + along_section(parts[step], step).astype(jnp.float32)
    return total


def tp_halves(total, tp):
    halves = total.reshape(total.shape[:3] + (TPS, PIECE // TPS) + total.shape[4:])
    keep = lax.dynamic_index_in_dim(halves, tp, 3, keepdims=False)
    give = lax.dynamic_index_in_dim(halves, 1 - tp, 3, keepdims=False)
    return keep, give.astype(jnp.bfloat16)


def tp_sums(keep, give):
    return keep + to_other_tp(give).astype(jnp.float32)


def row_stats(logits, columns, ids):
    picked = jnp.sum(jnp.where(columns == ids[..., None], logits, 0.0), axis=-1)
    row_top = jnp.max(logits, axis=-1)
    row_total = jnp.sum(jnp.exp(logits - row_top[..., None]), axis=-1)
    return jnp.stack([row_top, row_total, picked])


def cores_exchanged(array, axis, core):
    return jnp.where(core == 1, jnp.flip(array, axis), array)


def key_value_window(keys, values, segment_ids):
    id_row = jnp.concatenate([segment_ids, jnp.zeros_like(segment_ids)])[None, :]
    own = jnp.concatenate(
        [
            jnp.concatenate([keys, values], axis=1),
            jnp.broadcast_to(id_row.astype(jnp.bfloat16), (16, 2 * keys.shape[1])),
        ],
        axis=0,
    )[None]
    two = jnp.concatenate([passed_along(own, 1), own], axis=0)
    four = jnp.concatenate([passed_along(two, 2), two], axis=0)
    return jnp.concatenate([passed_along(own, 8), passed_along(four, 4), four], axis=0)


def body(
    teacher_hidden,
    lm_head,
    sampled_ids,
    student_logprob,
    owner_map,
    queries,
    keys,
    values,
    grad_out,
    segment_ids,
):
    ctx_index = lax.axis_index("ctx")
    section = lax.axis_index("section")
    tp = lax.axis_index("tp")
    place, core = lax.rem(ctx_index, Y * CORES), lax.rem(ctx_index, CORES)

    gathered = across_chips(teacher_hidden)
    window = key_value_window(keys, values, segment_ids)
    gathered, window = lax.optimization_barrier((gathered, window))
    logits = tp_sums(*tp_halves(section_sums(section_parts(gathered, lm_head, section)), tp))

    def kept(array, axis):
        return lax.dynamic_index_in_dim(
            lax.dynamic_index_in_dim(array, section, 0, keepdims=False), tp, axis, keepdims=False
        )

    def kept_rows(array):
        rows = kept(array.reshape(SECTIONS, 2, Y, CORES, TPS, PIECE // TPS), 3)
        return rows.transpose(2, 0, 1, 3)

    columns = ctx_index * lm_head.shape[1] + jnp.arange(lm_head.shape[1], dtype=jnp.int32)
    stats = row_stats(logits, columns, cores_exchanged(kept_rows(sampled_ids), 0, core))
    stats = cores_exchanged(stats, 1, core).reshape(3, -1)
    everywhere = lax.all_to_all(
        jnp.broadcast_to(stats, (Z * Y * CORES,) + stats.shape), "ctx", 0, 0
    )
    highest = jnp.max(everywhere[:, 0], axis=0)
    summed = jnp.sum(everywhere[:, 1] * jnp.exp(everywhere[:, 0] - highest), axis=0)
    teacher_logprob = jnp.sum(everywhere[:, 2], axis=0) - highest - jnp.log(summed)
    student_rows = kept_rows(student_logprob).reshape(-1)
    advantage = jnp.clip(teacher_logprob - student_rows, -clip_bound, clip_bound)
    count = SECTIONS * TPS
    everything = lax.all_to_all(
        jnp.broadcast_to(advantage, (count,) + advantage.shape), ("section", "tp"), 0, 0
    )
    owners = owner_map.reshape(SECTIONS, 2, Y, CORES, TPS, PIECE // TPS)
    owners = owners.transpose(0, 4, 3, 1, 2, 5).reshape(-1)
    advantage_own = everything.reshape(SECTIONS, TPS, CORES, 2, Y, PIECE // TPS)
    advantage_own = kept(advantage_own, 2).transpose(2, 1, 0, 3).reshape(-1)
    everything = everything.reshape(-1)

    seq_rows = queries.shape[0]
    head_dim = keys.shape[1]
    group = queries.shape[1] // head_dim
    scaling = head_dim ** (-0.5)
    query_position = ctx_index * seq_rows + jnp.arange(seq_rows, dtype=jnp.int32)
    routed = jnp.sum(
        jnp.where(owners[None, :] == query_position[:, None], everything[None, :], 0.0), axis=1
    )
    weight = 1.0 + advantage_scale * routed

    key_window = window[:, :seq_rows, :head_dim].reshape(-1, head_dim)
    value_window = window[:, :seq_rows, head_dim:].reshape(-1, head_dim)
    key_segment = window[:, seq_rows, :seq_rows].reshape(-1)
    key_position = (ctx_index - FARTHEST) * seq_rows + jnp.arange(
        (FARTHEST + 1) * seq_rows, dtype=jnp.int32
    )
    allowed = (
        (key_segment[None, :] == segment_ids.astype(jnp.bfloat16)[:, None])
        & (key_position[None, :] <= query_position[:, None])
        & (key_position[None, :] >= 0)
    )
    allowed = jnp.tile(allowed, (group, 1))

    def by_head(array):
        return (
            array.reshape(seq_rows, group, head_dim)
            .transpose(1, 0, 2)
            .reshape(group * seq_rows, head_dim)
        )

    query_rows, grad_rows = by_head(queries), by_head(grad_out)
    scores = jnp.dot(query_rows, key_window.T, preferred_element_type=jnp.float32) * scaling
    masked = jnp.where(allowed, scores, masked_value)
    top = jnp.max(masked, axis=1, keepdims=True)
    raised = jnp.where(allowed, jnp.exp(masked - top), 0.0)
    softmax = (raised / jnp.sum(raised, axis=1, keepdims=True)).astype(jnp.bfloat16)
    context = jnp.dot(softmax, value_window, preferred_element_type=jnp.float32)
    row_delta = jnp.sum(grad_rows.astype(jnp.float32) * context, axis=1, keepdims=True)
    grad_prob = jnp.dot(grad_rows, value_window.T, preferred_element_type=jnp.float32)
    grad_score = (softmax.astype(jnp.float32) * (grad_prob - row_delta) * scaling).astype(
        jnp.bfloat16
    )
    grad_query = jnp.dot(grad_score, key_window, preferred_element_type=jnp.float32)

    row_weight = jnp.tile(weight, (group,))[:, None]
    grad_query = (row_weight * grad_query).astype(jnp.bfloat16)
    weighted_query = (row_weight * query_rows.astype(jnp.float32)).astype(jnp.bfloat16)
    weighted_grad = (row_weight * grad_rows.astype(jnp.float32)).astype(jnp.bfloat16)
    grad_key = jnp.dot(grad_score.T, weighted_query, preferred_element_type=jnp.float32)
    grad_value = jnp.dot(softmax.T, weighted_grad, preferred_element_type=jnp.float32)
    both = jnp.concatenate([grad_key, grad_value], axis=1).reshape(
        FARTHEST + 1, seq_rows, 2 * head_dim
    )
    cyclic = both[1:].astype(jnp.bfloat16)
    cyclic = jnp.concatenate([cyclic, cyclic], axis=0)
    given = lax.dynamic_slice_in_dim(cyclic, Y * CORES - 1 - place, Y * CORES, 0)
    arrived = across_row(given).astype(jnp.float32)
    sender = jnp.arange(Y * CORES, dtype=jnp.int32)[:, None, None]
    back = both[0] + jnp.sum(jnp.where(sender < place, arrived, 0.0), axis=0)
    back = passed_along(back.astype(jnp.bfloat16), -Y * CORES).astype(jnp.float32)
    total = both[FARTHEST] + jnp.sum(jnp.where(sender > place, arrived, 0.0), axis=0) + back
    total = total.astype(jnp.bfloat16)
    d_queries = (
        grad_query.reshape(group, seq_rows, head_dim)
        .transpose(1, 0, 2)
        .reshape(seq_rows, group * head_dim)
    )
    return (advantage_own, d_queries, total[:, :head_dim], total[:, head_dim:])


def solution(mesh):
    in_specs = (
        P("ctx", ("section", "tp")),
        P(("section", "tp"), "ctx"),
        P(),
        P(),
        P(),
        P("ctx", ("section", "tp")),
        P("ctx", ("section", "tp")),
        P("ctx", ("section", "tp")),
        P("ctx", ("section", "tp")),
        P("ctx"),
    )
    out_specs = (
        P(("section", "tp")),
        P("ctx", ("section", "tp")),
        P("ctx", ("section", "tp")),
        P("ctx", ("section", "tp")),
    )
    return jax.shard_map(body, mesh=mesh, in_specs=in_specs, out_specs=out_specs, check_vma=False)
```

```python
import functools

import jax
import jax.numpy as jnp
from jax import lax
from jax.experimental import pallas as pl
from jax.experimental.pallas import tpu as pltpu
from jax.sharding import PartitionSpec as P

advantage_scale = 0.1
clip_bound = 8.0
masked_value = -1e30

Z, Y, CORES = 8, 4, 2
SECTIONS, TPS = 4, 2
PIECE = 16
FARTHEST = 8


def ctx_move(block, target):
    route = []
    for z in range(Z):
        for y in range(Y):
            for core in range(CORES):
                z2, y2, core2 = target(z, y, core)
                route.append(
                    (z * 8 + y * 2 + core, (z2 % Z) * 8 + (y2 % Y) * 2 + core2 % CORES)
                )
    return lax.ppermute(block, "ctx", route)


def copies_for_chips(block):
    return jnp.broadcast_to(block, (Z * Y,) + block.shape)


def across_chips(copies):
    groups = [[chip * CORES + core for chip in range(Z * Y)] for core in range(CORES)]
    return lax.all_to_all(copies, "ctx", 0, 0, axis_index_groups=groups)


def across_row(blocks):
    row = Y * CORES
    groups = [[z * row + place for place in range(row)] for z in range(Z)]
    return lax.all_to_all(blocks, "ctx", 0, 0, axis_index_groups=groups)


def other_core(block):
    return ctx_move(block, lambda z, y, core: (z, y, core + 1))


def passed_along(block, distance):
    count = Z * Y * CORES
    route = [(i - distance, i) for i in range(count) if 0 <= i - distance < count]
    return lax.ppermute(block, "ctx", route)


def along_section(block, step):
    return lax.ppermute(block, "section", [(s, (s + step) % SECTIONS) for s in range(SECTIONS)])


def to_other_tp(block):
    return lax.ppermute(block, "tp", [(0, 1), (1, 0)])


def logits_kernel(section_ref, mine_ref, theirs_ref, head_ref, *refs):
    outs, logits = refs[:SECTIONS], refs[SECTIONS]
    count = outs[0].shape[1]
    for part, rows in enumerate((mine_ref, theirs_ref)):
        logits[part] = jnp.dot(rows[...], head_ref[...], preferred_element_type=jnp.float32)
        for step, out in enumerate(outs):
            place = lax.rem(section_ref[0] + step, SECTIONS)
            kept = logits[part, pl.ds(pl.multiple_of(place * count, count), count), :]
            out[part] = kept.astype(out.dtype)


def section_parts(gathered, weight, section):
    mine = gathered.reshape(-1, gathered.shape[2])
    rows, depth = mine.shape
    vocab, tile = weight.shape[1], 256
    count = rows // SECTIONS
    whole = pl.BlockSpec((rows, depth), lambda n: (0, 0))
    kinds = [jnp.float32] + [jnp.bfloat16] * (SECTIONS - 1)
    return pl.pallas_call(
        logits_kernel,
        grid=(vocab // tile,),
        in_specs=[
            pl.BlockSpec(memory_space=pltpu.SMEM),
            whole,
            whole,
            pl.BlockSpec((depth, tile), lambda n: (0, n)),
        ],
        out_specs=[pl.BlockSpec((2, count, tile), lambda n: (0, 0, n))] * SECTIONS,
        out_shape=[jax.ShapeDtypeStruct((2, count, vocab), kind) for kind in kinds],
        scratch_shapes=[pltpu.VMEM((2, rows, tile), jnp.float32)],
        compiler_params=pltpu.CompilerParams(vmem_limit_bytes=24 * 1024 * 1024),
        cost_estimate=pl.CostEstimate(
            flops=4 * rows * depth * vocab,
            bytes_accessed=2 * depth * vocab + 4 * rows * depth + 5 * rows * vocab,
            transcendentals=0,
        ),
    )(jnp.reshape(section, (1,)), mine, other_core(mine), weight)


def section_arrivals(parts):
    return [along_section(parts[step], step) for step in (1, 2, 3)]


def section_sums(own, arrivals):
    return functools.reduce(lambda total, part: total + part.astype(jnp.float32), arrivals, own)


def tp_halves(total, tp):
    halves = total.reshape(2, TPS, -1, total.shape[2])
    keep = lax.dynamic_index_in_dim(halves, tp, 1, keepdims=False)
    give = lax.dynamic_index_in_dim(halves, 1 - tp, 1, keepdims=False)
    return keep, give.astype(jnp.bfloat16)


def tp_sums(keep, give):
    return keep + to_other_tp(give).astype(jnp.float32)


def row_stats(logits, columns, ids):
    picked = jnp.sum(jnp.where(columns == ids[..., None], logits, 0.0), axis=-1)
    row_top = jnp.max(logits, axis=-1)
    row_total = jnp.sum(jnp.exp(logits - row_top[..., None]), axis=-1)
    return jnp.stack([row_top, row_total, picked])


def cores_exchanged(array, axis, core):
    return jnp.where(core == 1, jnp.flip(array, axis), array)


def packed_window(keys, values, segment_ids):
    id_row = jnp.concatenate([segment_ids, jnp.zeros_like(segment_ids)])[None, :]
    return jnp.concatenate(
        [
            jnp.concatenate([keys, values], axis=1),
            jnp.broadcast_to(id_row.astype(jnp.bfloat16), (16, 2 * keys.shape[1])),
        ],
        axis=0,
    )[None]


def body(
    teacher_hidden,
    lm_head,
    sampled_ids,
    student_logprob,
    owner_map,
    queries,
    keys,
    values,
    grad_out,
    segment_ids,
):
    ctx_index = lax.axis_index("ctx")
    section = lax.axis_index("section")
    tp = lax.axis_index("tp")
    place, core = lax.rem(ctx_index, Y * CORES), lax.rem(ctx_index, CORES)

    half = teacher_hidden.shape[0] // 2
    first = across_chips(copies_for_chips(teacher_hidden[:half]))
    copies = copies_for_chips(teacher_hidden[half:])
    own_window = packed_window(keys, values, segment_ids)
    eighth = passed_along(own_window, 8)
    two_windows = jnp.concatenate([passed_along(own_window, 1), own_window], axis=0)
    first, copies, eighth, two_windows = lax.optimization_barrier(
        (first, copies, eighth, two_windows)
    )
    last = across_chips(copies)
    first = section_parts(first, lm_head, section)
    arrivals = section_arrivals(first)
    arrivals[2], two_windows = lax.optimization_barrier((arrivals[2], two_windows))
    four_windows = jnp.concatenate([passed_along(two_windows, 2), two_windows], axis=0)
    first, last = lax.optimization_barrier((section_sums(first[0], arrivals), last))
    keep, give = tp_halves(first, tp)
    last = section_parts(last, lm_head, section)
    give, last = lax.optimization_barrier((give, last))
    arrivals = section_arrivals(last)
    first = tp_sums(keep, give)
    last, four_windows = lax.optimization_barrier((section_sums(last[0], arrivals), four_windows))
    last = tp_sums(*tp_halves(last, tp))
    window = jnp.concatenate([eighth, passed_along(four_windows, 4), four_windows], axis=0)

    def kept_rows(array):
        rows = array.reshape(SECTIONS * TPS, Y, CORES, 2, half)
        return lax.dynamic_index_in_dim(
            rows, section * TPS + tp, 0, keepdims=False
        ).transpose(1, 0, 2, 3)

    logits = jnp.stack(
        [part.reshape(CORES, Y, half, -1) for part in (first, last)], axis=2
    )
    columns = ctx_index * lm_head.shape[1] + jnp.arange(lm_head.shape[1], dtype=jnp.int32)
    stats = row_stats(logits, columns, cores_exchanged(kept_rows(sampled_ids), 0, core))
    stats = cores_exchanged(stats, 1, core).reshape(3, -1)
    everywhere = lax.all_to_all(
        jnp.broadcast_to(stats, (Z * Y * CORES,) + stats.shape), "ctx", 0, 0
    )
    highest = jnp.max(everywhere[:, 0], axis=0)
    summed = jnp.sum(everywhere[:, 1] * jnp.exp(everywhere[:, 0] - highest), axis=0)
    teacher_logprob = jnp.sum(everywhere[:, 2], axis=0) - highest - jnp.log(summed)
    student_rows = kept_rows(student_logprob).reshape(-1)
    advantage = jnp.clip(teacher_logprob - student_rows, -clip_bound, clip_bound)
    count = SECTIONS * TPS
    everything = lax.all_to_all(
        jnp.broadcast_to(advantage, (count,) + advantage.shape), ("section", "tp"), 0, 0
    )
    owners = owner_map.reshape(SECTIONS * TPS, Y, CORES, PIECE).transpose(0, 2, 1, 3).reshape(-1)
    advantage_own = advantage.reshape(CORES, Y, PIECE).transpose(1, 0, 2).reshape(-1)
    everything = everything.reshape(-1)

    seq_rows = queries.shape[0]
    head_dim = keys.shape[1]
    group = queries.shape[1] // head_dim
    scaling = head_dim ** (-0.5)
    query_position = ctx_index * seq_rows + jnp.arange(seq_rows, dtype=jnp.int32)
    routed = jnp.sum(
        jnp.where(owners[None, :] == query_position[:, None], everything[None, :], 0.0), axis=1
    )
    weight = 1.0 + advantage_scale * routed

    key_window = window[:, :seq_rows, :head_dim].reshape(-1, head_dim)
    value_window = window[:, :seq_rows, head_dim:].reshape(-1, head_dim)
    key_segment = window[:, seq_rows, :seq_rows].reshape(-1)
    key_position = (ctx_index - FARTHEST) * seq_rows + jnp.arange(
        (FARTHEST + 1) * seq_rows, dtype=jnp.int32
    )
    allowed = (
        (key_segment[None, :] == segment_ids.astype(jnp.bfloat16)[:, None])
        & (key_position[None, :] <= query_position[:, None])
        & (key_position[None, :] >= 0)
    )
    allowed = jnp.tile(allowed, (group, 1))

    def by_head(array):
        return (
            array.reshape(seq_rows, group, head_dim)
            .transpose(1, 0, 2)
            .reshape(group * seq_rows, head_dim)
        )

    query_rows, grad_rows = by_head(queries), by_head(grad_out)
    scores = jnp.dot(query_rows, key_window.T, preferred_element_type=jnp.float32) * scaling
    masked = jnp.where(allowed, scores, masked_value)
    top = jnp.max(masked, axis=1, keepdims=True)
    raised = jnp.where(allowed, jnp.exp(masked - top), 0.0)
    softmax = (raised / jnp.sum(raised, axis=1, keepdims=True)).astype(jnp.bfloat16)
    context = jnp.dot(softmax, value_window, preferred_element_type=jnp.float32)
    row_delta = jnp.sum(grad_rows.astype(jnp.float32) * context, axis=1, keepdims=True)
    grad_prob = jnp.dot(grad_rows, value_window.T, preferred_element_type=jnp.float32)
    grad_score = (softmax.astype(jnp.float32) * (grad_prob - row_delta) * scaling).astype(
        jnp.bfloat16
    )
    grad_query = jnp.dot(grad_score, key_window, preferred_element_type=jnp.float32)

    row_weight = jnp.tile(weight, (group,))[:, None]
    grad_query = (row_weight * grad_query).astype(jnp.bfloat16)
    weighted_query = (row_weight * query_rows.astype(jnp.float32)).astype(jnp.bfloat16)
    weighted_grad = (row_weight * grad_rows.astype(jnp.float32)).astype(jnp.bfloat16)
    grad_key = jnp.dot(grad_score.T, weighted_query, preferred_element_type=jnp.float32)
    grad_value = jnp.dot(softmax.T, weighted_grad, preferred_element_type=jnp.float32)
    both = jnp.concatenate([grad_key, grad_value], axis=1).reshape(
        FARTHEST + 1, seq_rows, 2 * head_dim
    )
    d_queries = (
        grad_query.reshape(group, seq_rows, head_dim)
        .transpose(1, 0, 2)
        .reshape(seq_rows, group * head_dim)
    )
    cyclic = both[1:].astype(jnp.bfloat16)
    cyclic = jnp.concatenate([cyclic, cyclic], axis=0)
    given = lax.dynamic_slice_in_dim(cyclic, Y * CORES - 1 - place, Y * CORES, 0)
    arrived, d_queries = lax.optimization_barrier((across_row(given), d_queries))
    arrived = arrived.astype(jnp.float32)
    sender = jnp.arange(Y * CORES, dtype=jnp.int32)[:, None, None]
    back = both[0] + jnp.sum(jnp.where(sender < place, arrived, 0.0), axis=0)
    back = passed_along(back.astype(jnp.bfloat16), -Y * CORES).astype(jnp.float32)
    here = both[FARTHEST] + jnp.sum(jnp.where(sender > place, arrived, 0.0), axis=0)
    d_keys = (here[:, :head_dim] + back[:, :head_dim]).astype(jnp.bfloat16)
    d_values = (here[:, head_dim:] + back[:, head_dim:]).astype(jnp.bfloat16)
    return (advantage_own, d_queries, d_keys, d_values)


def solution(mesh):
    in_specs = (
        P("ctx", ("section", "tp")),
        P(("section", "tp"), "ctx"),
        P(),
        P(),
        P(),
        P("ctx", ("section", "tp")),
        P("ctx", ("section", "tp")),
        P("ctx", ("section", "tp")),
        P("ctx", ("section", "tp")),
        P("ctx"),
    )
    out_specs = (
        P(("section", "tp")),
        P("ctx", ("section", "tp")),
        P("ctx", ("section", "tp")),
        P("ctx", ("section", "tp")),
    )
    return jax.shard_map(body, mesh=mesh, in_specs=in_specs, out_specs=out_specs, check_vma=False)
```

```python
import jax
import jax.numpy as jnp
from jax import lax
from jax.sharding import PartitionSpec as P

advantage_scale = 0.1
clip_bound = 8.0
masked_value = -1e30

Z, Y, CORES = 8, 4, 2
SECTIONS, TPS = 4, 2
PIECE = 16
FARTHEST = 8


def ctx_move(block, target):
    route = []
    for z in range(Z):
        for y in range(Y):
            for core in range(CORES):
                z2, y2, core2 = target(z, y, core)
                route.append(
                    (z * 8 + y * 2 + core, (z2 % Z) * 8 + (y2 % Y) * 2 + core2 % CORES)
                )
    return lax.ppermute(block, "ctx", route)


def copies_for_chips(block):
    return jnp.broadcast_to(block, (Z * Y,) + block.shape)


def across_chips(copies):
    groups = [[chip * CORES + core for chip in range(Z * Y)] for core in range(CORES)]
    return lax.all_to_all(copies, "ctx", 0, 0, axis_index_groups=groups)


def across_row(blocks):
    row = Y * CORES
    groups = [[z * row + place for place in range(row)] for z in range(Z)]
    return lax.all_to_all(blocks, "ctx", 0, 0, axis_index_groups=groups)


def other_core(block):
    return ctx_move(block, lambda z, y, core: (z, y, core + 1))


def passed_along(block, distance):
    count = Z * Y * CORES
    route = [(i - distance, i) for i in range(count) if 0 <= i - distance < count]
    return lax.ppermute(block, "ctx", route)


def over_section(block, bits):
    return lax.ppermute(block, "section", [(s, s ^ bits) for s in range(SECTIONS)])


def to_other_tp(block):
    return lax.ppermute(block, "tp", [(0, 1), (1, 0)])


def both_logits(gathered, weight):
    mine = gathered.reshape(-1, gathered.shape[2])
    for rows in (mine, other_core(mine)):
        logits = jnp.dot(rows, weight, preferred_element_type=jnp.float32)
        yield logits.reshape(SECTIONS, TPS, Y, gathered.shape[1], weight.shape[1])


def of_section(logits, section):
    return lax.dynamic_index_in_dim(logits, section, 0, keepdims=False)


def first_round(logits, section, bits):
    given = jnp.stack([of_section(logits, section ^ bits), of_section(logits, section ^ 2)])
    return over_section(given.astype(jnp.bfloat16), bits)


def second_round(logits, arrived, section, bits):
    arrived = arrived.astype(jnp.float32)
    given = of_section(logits, section ^ bits) + arrived[1]
    return of_section(logits, section) + arrived[0] + over_section(
        given.astype(jnp.bfloat16), bits
    ).astype(jnp.float32)


def tp_halves(total, tp):
    keep = lax.dynamic_index_in_dim(total, tp, 1, keepdims=False)
    give = lax.dynamic_index_in_dim(total, 1 - tp, 1, keepdims=False)
    return keep, give.astype(jnp.bfloat16)


def tp_sums(keep, give):
    return keep + to_other_tp(give).astype(jnp.float32)


def row_stats(logits, columns, ids):
    picked = jnp.sum(jnp.where(columns == ids[..., None], logits, 0.0), axis=-1)
    row_top = jnp.max(logits, axis=-1)
    row_total = jnp.sum(jnp.exp(logits - row_top[..., None]), axis=-1)
    return jnp.stack([row_top, row_total, picked])


def cores_exchanged(array, axis, core):
    return jnp.where(core == 1, jnp.flip(array, axis), array)


def packed_window(keys, values, segment_ids):
    id_row = jnp.concatenate([segment_ids, jnp.zeros_like(segment_ids)])[None, :]
    return jnp.concatenate(
        [
            jnp.concatenate([keys, values], axis=1),
            jnp.broadcast_to(id_row.astype(jnp.bfloat16), (16, 2 * keys.shape[1])),
        ],
        axis=0,
    )[None]


def body(
    teacher_hidden,
    lm_head,
    sampled_ids,
    student_logprob,
    owner_map,
    queries,
    keys,
    values,
    grad_out,
    segment_ids,
):
    ctx_index = lax.axis_index("ctx")
    section = lax.axis_index("section")
    tp = lax.axis_index("tp")
    place, core = lax.rem(ctx_index, Y * CORES), lax.rem(ctx_index, CORES)

    seq_rows = queries.shape[0]
    head_dim = keys.shape[1]
    group = queries.shape[1] // head_dim
    scaling = head_dim ** (-0.5)

    query_position = ctx_index * seq_rows + jnp.arange(seq_rows, dtype=jnp.int32)
    key_position = (ctx_index - FARTHEST) * seq_rows + jnp.arange(
        (FARTHEST + 1) * seq_rows, dtype=jnp.int32
    )
    reached = (key_position[None, :] <= query_position[:, None]) & (key_position[None, :] >= 0)
    owners = owner_map.reshape(SECTIONS * TPS, Y, CORES, PIECE).transpose(0, 2, 1, 3).reshape(-1)
    routes = owners[None, :] == query_position[:, None]

    def by_head(array):
        return (
            array.reshape(seq_rows, group, head_dim)
            .transpose(1, 0, 2)
            .reshape(group * seq_rows, head_dim)
        )

    query_rows, grad_rows = by_head(queries), by_head(grad_out)
    own_window = packed_window(keys, values, segment_ids)
    eighth = passed_along(own_window, 8)
    two_windows = jnp.concatenate([passed_along(own_window, 1), own_window], axis=0)

    half = teacher_hidden.shape[0] // 2
    first = across_chips(copies_for_chips(teacher_hidden[:half]))
    copies = copies_for_chips(teacher_hidden[half:])
    (
        first, copies, eighth, two_windows, query_rows, grad_rows, reached, routes,
    ) = lax.optimization_barrier(
        (first, copies, eighth, two_windows, query_rows, grad_rows, reached, routes)
    )
    last = across_chips(copies)
    mine, theirs = both_logits(first, lm_head)
    arrived = [first_round(mine, section, 1), first_round(theirs, section, 3)]
    arrived[1], two_windows = lax.optimization_barrier((arrived[1], two_windows))
    four_windows = jnp.concatenate([passed_along(two_windows, 2), two_windows], axis=0)
    first = jnp.stack(
        [
            second_round(mine, arrived[0], section, 3),
            second_round(theirs, arrived[1], section, 1),
        ]
    )
    first, last, four_windows = lax.optimization_barrier((first, last, four_windows))
    first = tp_sums(*tp_halves(first, tp))
    mine, theirs = both_logits(last, lm_head)
    arrived = [first_round(mine, section, 1), first_round(theirs, section, 3)]
    arrived[0], first = lax.optimization_barrier((arrived[0], first))
    last = jnp.stack(
        [
            second_round(mine, arrived[0], section, 3),
            second_round(theirs, arrived[1], section, 1),
        ]
    )
    last, four_windows = lax.optimization_barrier((last, four_windows))
    last = tp_sums(*tp_halves(last, tp))
    window = jnp.concatenate([eighth, passed_along(four_windows, 4), four_windows], axis=0)

    def kept_rows(array):
        rows = array.reshape(SECTIONS * TPS, Y, CORES, 2, half)
        return lax.dynamic_index_in_dim(
            rows, section * TPS + tp, 0, keepdims=False
        ).transpose(1, 0, 2, 3)

    logits = jnp.stack([first, last], axis=2)
    columns = ctx_index * lm_head.shape[1] + jnp.arange(lm_head.shape[1], dtype=jnp.int32)
    stats = row_stats(logits, columns, cores_exchanged(kept_rows(sampled_ids), 0, core))
    stats = cores_exchanged(stats, 1, core).reshape(3, -1)
    everywhere = lax.all_to_all(
        jnp.broadcast_to(stats, (Z * Y * CORES,) + stats.shape), "ctx", 0, 0
    )
    highest = jnp.max(everywhere[:, 0], axis=0)
    summed = jnp.sum(everywhere[:, 1] * jnp.exp(everywhere[:, 0] - highest), axis=0)
    teacher_logprob = jnp.sum(everywhere[:, 2], axis=0) - highest - jnp.log(summed)
    student_rows = kept_rows(student_logprob).reshape(-1)
    advantage = jnp.clip(teacher_logprob - student_rows, -clip_bound, clip_bound)
    count = SECTIONS * TPS
    everything = lax.all_to_all(
        jnp.broadcast_to(advantage, (count,) + advantage.shape), ("section", "tp"), 0, 0
    )
    advantage_own = advantage.reshape(CORES, Y, PIECE).transpose(1, 0, 2).reshape(-1)
    everything = everything.reshape(-1)

    routed = jnp.sum(jnp.where(routes, everything[None, :], 0.0), axis=1)
    weight = 1.0 + advantage_scale * routed

    key_window = window[:, :seq_rows, :head_dim].reshape(-1, head_dim)
    value_window = window[:, :seq_rows, head_dim:].reshape(-1, head_dim)
    key_segment = window[:, seq_rows, :seq_rows].reshape(-1)
    own_segment = segment_ids.astype(jnp.bfloat16)
    allowed = (key_segment[None, :] == own_segment[:, None]) & reached
    allowed = jnp.tile(allowed, (group, 1))

    scores = jnp.dot(query_rows, key_window.T, preferred_element_type=jnp.float32) * scaling
    masked = jnp.where(allowed, scores, masked_value)
    top = jnp.max(masked, axis=1, keepdims=True)
    raised = jnp.where(allowed, jnp.exp(masked - top), 0.0)
    softmax = (raised / jnp.sum(raised, axis=1, keepdims=True)).astype(jnp.bfloat16)
    context = jnp.dot(softmax, value_window, preferred_element_type=jnp.float32)
    row_delta = jnp.sum(grad_rows.astype(jnp.float32) * context, axis=1, keepdims=True)
    grad_prob = jnp.dot(grad_rows, value_window.T, preferred_element_type=jnp.float32)
    grad_score = (softmax.astype(jnp.float32) * (grad_prob - row_delta) * scaling).astype(
        jnp.bfloat16
    )
    grad_query = jnp.dot(grad_score, key_window, preferred_element_type=jnp.float32)

    row_weight = jnp.tile(weight, (group,))[:, None]
    grad_query = (row_weight * grad_query).astype(jnp.bfloat16)
    weighted_query = (row_weight * query_rows.astype(jnp.float32)).astype(jnp.bfloat16)
    weighted_grad = (row_weight * grad_rows.astype(jnp.float32)).astype(jnp.bfloat16)
    grad_key = jnp.dot(grad_score.T, weighted_query, preferred_element_type=jnp.float32)
    grad_value = jnp.dot(softmax.T, weighted_grad, preferred_element_type=jnp.float32)
    both = jnp.concatenate([grad_key, grad_value], axis=1).reshape(
        FARTHEST + 1, seq_rows, 2 * head_dim
    )
    d_queries = (
        grad_query.reshape(group, seq_rows, head_dim)
        .transpose(1, 0, 2)
        .reshape(seq_rows, group * head_dim)
    )
    cyclic = both[1:].astype(jnp.bfloat16)
    cyclic = jnp.concatenate([cyclic, cyclic], axis=0)
    given = lax.dynamic_slice_in_dim(cyclic, Y * CORES - 1 - place, Y * CORES, 0)
    arrived, d_queries = lax.optimization_barrier((across_row(given), d_queries))
    arrived = arrived.astype(jnp.float32)
    sender = jnp.arange(Y * CORES, dtype=jnp.int32)[:, None, None]
    back = both[0] + jnp.sum(jnp.where(sender < place, arrived, 0.0), axis=0)
    back = passed_along(back.astype(jnp.bfloat16), -Y * CORES).astype(jnp.float32)
    here = both[FARTHEST] + jnp.sum(jnp.where(sender > place, arrived, 0.0), axis=0)
    d_keys = (here[:, :head_dim] + back[:, :head_dim]).astype(jnp.bfloat16)
    d_values = (here[:, head_dim:] + back[:, head_dim:]).astype(jnp.bfloat16)
    return (advantage_own, d_queries, d_keys, d_values)


def solution(mesh):
    in_specs = (
        P("ctx", ("section", "tp")),
        P(("section", "tp"), "ctx"),
        P(),
        P(),
        P(),
        P("ctx", ("section", "tp")),
        P("ctx", ("section", "tp")),
        P("ctx", ("section", "tp")),
        P("ctx", ("section", "tp")),
        P("ctx"),
    )
    out_specs = (
        P(("section", "tp")),
        P("ctx", ("section", "tp")),
        P("ctx", ("section", "tp")),
        P("ctx", ("section", "tp")),
    )
    return jax.shard_map(body, mesh=mesh, in_specs=in_specs, out_specs=out_specs, check_vma=False)
```

```python
import functools

import jax
import jax.numpy as jnp
from jax import lax
from jax.sharding import PartitionSpec as P

advantage_scale = 0.1
clip_bound = 8.0
masked_value = -1e30

Z, Y, CORES = 8, 4, 2
SECTIONS, TPS = 4, 2
PIECE = 16
FARTHEST = 8


def ctx_move(block, target):
    route = []
    for z in range(Z):
        for y in range(Y):
            for core in range(CORES):
                z2, y2, core2 = target(z, y, core)
                route.append(
                    (z * 8 + y * 2 + core, (z2 % Z) * 8 + (y2 % Y) * 2 + core2 % CORES)
                )
    return lax.ppermute(block, "ctx", route)


def copies_for_chips(block):
    return jnp.broadcast_to(block, (Z * Y,) + block.shape)


def across_chips(copies):
    groups = [[chip * CORES + core for chip in range(Z * Y)] for core in range(CORES)]
    return lax.all_to_all(copies, "ctx", 0, 0, axis_index_groups=groups)


def across_row(blocks):
    row = Y * CORES
    groups = [[z * row + place for place in range(row)] for z in range(Z)]
    return lax.all_to_all(blocks, "ctx", 0, 0, axis_index_groups=groups)


def other_core(block):
    return ctx_move(block, lambda z, y, core: (z, y, core + 1))


def passed_along(block, distance):
    count = Z * Y * CORES
    route = [(i - distance, i) for i in range(count) if 0 <= i - distance < count]
    return lax.ppermute(block, "ctx", route)


def along_section(block, step):
    return lax.ppermute(block, "section", [(s, (s + step) % SECTIONS) for s in range(SECTIONS)])


def to_other_tp(block):
    return lax.ppermute(block, "tp", [(0, 1), (1, 0)])


def section_parts(gathered, weight, section):
    mine = gathered.reshape(-1, gathered.shape[2])
    parts = []
    for rows in (mine, other_core(mine)):
        part = jnp.dot(rows, weight, preferred_element_type=jnp.float32)
        parts.append(part.reshape(SECTIONS, TPS, Y, gathered.shape[1], weight.shape[1]))

    def rows_for(step):
        place = lax.rem(section + step, SECTIONS)
        return jnp.stack(
            [lax.dynamic_index_in_dim(part, place, 0, keepdims=False) for part in parts]
        )

    return [rows_for(0)] + [rows_for(step).astype(jnp.bfloat16) for step in (1, 2, 3)]


def section_arrivals(parts):
    return [along_section(parts[step], step) for step in (1, 2, 3)]


def section_sums(own, arrivals):
    return functools.reduce(lambda total, part: total + part.astype(jnp.float32), arrivals, own)


def tp_halves(total, tp):
    keep = lax.dynamic_index_in_dim(total, tp, 1, keepdims=False)
    give = lax.dynamic_index_in_dim(total, 1 - tp, 1, keepdims=False)
    return keep, give.astype(jnp.bfloat16)


def tp_sums(keep, give):
    return keep + to_other_tp(give).astype(jnp.float32)


def row_stats(logits, columns, ids):
    picked = jnp.sum(jnp.where(columns == ids[..., None], logits, 0.0), axis=-1)
    row_top = jnp.max(logits, axis=-1)
    row_total = jnp.sum(jnp.exp(logits - row_top[..., None]), axis=-1)
    return jnp.stack([row_top, row_total, picked])


def cores_exchanged(array, axis, core):
    return jnp.where(core == 1, jnp.flip(array, axis), array)


def packed_window(keys, values, segment_ids):
    id_row = jnp.concatenate([segment_ids, jnp.zeros_like(segment_ids)])[None, :]
    return jnp.concatenate(
        [
            jnp.concatenate([keys, values], axis=1),
            jnp.broadcast_to(id_row.astype(jnp.bfloat16), (16, 2 * keys.shape[1])),
        ],
        axis=0,
    )[None]


def body(
    teacher_hidden,
    lm_head,
    sampled_ids,
    student_logprob,
    owner_map,
    queries,
    keys,
    values,
    grad_out,
    segment_ids,
):
    ctx_index = lax.axis_index("ctx")
    section = lax.axis_index("section")
    tp = lax.axis_index("tp")
    place, core = lax.rem(ctx_index, Y * CORES), lax.rem(ctx_index, CORES)

    half = teacher_hidden.shape[0] // 2
    first = across_chips(copies_for_chips(teacher_hidden[:half]))
    copies = copies_for_chips(teacher_hidden[half:])
    own_window = packed_window(keys, values, segment_ids)
    eighth = passed_along(own_window, 8)
    two_windows = jnp.concatenate([passed_along(own_window, 1), own_window], axis=0)
    first, copies, eighth, two_windows = lax.optimization_barrier(
        (first, copies, eighth, two_windows)
    )
    last = across_chips(copies)
    first = section_parts(first, lm_head, section)
    arrivals = section_arrivals(first)
    arrivals[2], two_windows = lax.optimization_barrier((arrivals[2], two_windows))
    four_windows = jnp.concatenate([passed_along(two_windows, 2), two_windows], axis=0)
    first, last, four_windows = lax.optimization_barrier(
        (section_sums(first[0], arrivals), last, four_windows)
    )
    keep, give = tp_halves(first, tp)
    last = section_parts(last, lm_head, section)
    give, last = lax.optimization_barrier((give, last))
    first = tp_sums(keep, give)
    last, four_windows = lax.optimization_barrier(
        (section_sums(last[0], section_arrivals(last)), four_windows)
    )
    last = tp_sums(*tp_halves(last, tp))
    window = jnp.concatenate([eighth, passed_along(four_windows, 4), four_windows], axis=0)

    def kept_rows(array):
        rows = array.reshape(SECTIONS * TPS, Y, CORES, 2, half)
        return lax.dynamic_index_in_dim(
            rows, section * TPS + tp, 0, keepdims=False
        ).transpose(1, 0, 2, 3)

    logits = jnp.stack([first, last], axis=2)
    columns = ctx_index * lm_head.shape[1] + jnp.arange(lm_head.shape[1], dtype=jnp.int32)
    stats = row_stats(logits, columns, cores_exchanged(kept_rows(sampled_ids), 0, core))
    stats = cores_exchanged(stats, 1, core).reshape(3, -1)
    everywhere = lax.all_to_all(
        jnp.broadcast_to(stats, (Z * Y * CORES,) + stats.shape), "ctx", 0, 0
    )
    highest = jnp.max(everywhere[:, 0], axis=0)
    summed = jnp.sum(everywhere[:, 1] * jnp.exp(everywhere[:, 0] - highest), axis=0)
    teacher_logprob = jnp.sum(everywhere[:, 2], axis=0) - highest - jnp.log(summed)
    student_rows = kept_rows(student_logprob).reshape(-1)
    advantage = jnp.clip(teacher_logprob - student_rows, -clip_bound, clip_bound)
    count = SECTIONS * TPS
    everything = lax.all_to_all(
        jnp.broadcast_to(advantage, (count,) + advantage.shape), ("section", "tp"), 0, 0
    )
    owners = owner_map.reshape(SECTIONS * TPS, Y, CORES, PIECE).transpose(0, 2, 1, 3).reshape(-1)
    advantage_own = advantage.reshape(CORES, Y, PIECE).transpose(1, 0, 2).reshape(-1)
    everything = everything.reshape(-1)

    seq_rows = queries.shape[0]
    head_dim = keys.shape[1]
    group = queries.shape[1] // head_dim
    scaling = head_dim ** (-0.5)
    query_position = ctx_index * seq_rows + jnp.arange(seq_rows, dtype=jnp.int32)
    routed = jnp.sum(
        jnp.where(owners[None, :] == query_position[:, None], everything[None, :], 0.0), axis=1
    )
    weight = 1.0 + advantage_scale * routed

    key_window = window[:, :seq_rows, :head_dim].reshape(-1, head_dim)
    value_window = window[:, :seq_rows, head_dim:].reshape(-1, head_dim)
    key_segment = window[:, seq_rows, :seq_rows].reshape(-1)
    key_position = (ctx_index - FARTHEST) * seq_rows + jnp.arange(
        (FARTHEST + 1) * seq_rows, dtype=jnp.int32
    )
    allowed = (
        (key_segment[None, :] == segment_ids.astype(jnp.bfloat16)[:, None])
        & (key_position[None, :] <= query_position[:, None])
        & (key_position[None, :] >= 0)
    )
    allowed = jnp.tile(allowed, (group, 1))

    def by_head(array):
        return (
            array.reshape(seq_rows, group, head_dim)
            .transpose(1, 0, 2)
            .reshape(group * seq_rows, head_dim)
        )

    query_rows, grad_rows = by_head(queries), by_head(grad_out)
    scores = jnp.dot(query_rows, key_window.T, preferred_element_type=jnp.float32) * scaling
    masked = jnp.where(allowed, scores, masked_value)
    top = jnp.max(masked, axis=1, keepdims=True)
    raised = jnp.where(allowed, jnp.exp(masked - top), 0.0)
    softmax = (raised / jnp.sum(raised, axis=1, keepdims=True)).astype(jnp.bfloat16)
    context = jnp.dot(softmax, value_window, preferred_element_type=jnp.float32)
    row_delta = jnp.sum(grad_rows.astype(jnp.float32) * context, axis=1, keepdims=True)
    grad_prob = jnp.dot(grad_rows, value_window.T, preferred_element_type=jnp.float32)
    grad_score = (softmax.astype(jnp.float32) * (grad_prob - row_delta) * scaling).astype(
        jnp.bfloat16
    )
    grad_query = jnp.dot(grad_score, key_window, preferred_element_type=jnp.float32)

    row_weight = jnp.tile(weight, (group,))[:, None]
    grad_query = (row_weight * grad_query).astype(jnp.bfloat16)
    weighted_query = (row_weight * query_rows.astype(jnp.float32)).astype(jnp.bfloat16)
    weighted_grad = (row_weight * grad_rows.astype(jnp.float32)).astype(jnp.bfloat16)
    grad_key = jnp.dot(grad_score.T, weighted_query, preferred_element_type=jnp.float32)
    grad_value = jnp.dot(softmax.T, weighted_grad, preferred_element_type=jnp.float32)
    both = jnp.concatenate([grad_key, grad_value], axis=1).reshape(
        FARTHEST + 1, seq_rows, 2 * head_dim
    )
    cyclic = both[1:].astype(jnp.bfloat16)
    cyclic = jnp.concatenate([cyclic, cyclic], axis=0)
    given = lax.dynamic_slice_in_dim(cyclic, Y * CORES - 1 - place, Y * CORES, 0)
    arrived = across_row(given).astype(jnp.float32)
    sender = jnp.arange(Y * CORES, dtype=jnp.int32)[:, None, None]
    back = both[0] + jnp.sum(jnp.where(sender < place, arrived, 0.0), axis=0)
    back = passed_along(back.astype(jnp.bfloat16), -Y * CORES).astype(jnp.float32)
    here = both[FARTHEST] + jnp.sum(jnp.where(sender > place, arrived, 0.0), axis=0)
    d_keys = (here[:, :head_dim] + back[:, :head_dim]).astype(jnp.bfloat16)
    d_values = (here[:, head_dim:] + back[:, head_dim:]).astype(jnp.bfloat16)
    d_queries = (
        grad_query.reshape(group, seq_rows, head_dim)
        .transpose(1, 0, 2)
        .reshape(seq_rows, group * head_dim)
    )
    return (advantage_own, d_queries, d_keys, d_values)


def solution(mesh):
    in_specs = (
        P("ctx", ("section", "tp")),
        P(("section", "tp"), "ctx"),
        P(),
        P(),
        P(),
        P("ctx", ("section", "tp")),
        P("ctx", ("section", "tp")),
        P("ctx", ("section", "tp")),
        P("ctx", ("section", "tp")),
        P("ctx"),
    )
    out_specs = (
        P(("section", "tp")),
        P("ctx", ("section", "tp")),
        P("ctx", ("section", "tp")),
        P("ctx", ("section", "tp")),
    )
    return jax.shard_map(body, mesh=mesh, in_specs=in_specs, out_specs=out_specs, check_vma=False)
```

```python
import functools

import jax
import jax.numpy as jnp
from jax import lax
from jax.sharding import PartitionSpec as P

advantage_scale = 0.1
clip_bound = 8.0
masked_value = -1e30

Z, Y, CORES = 8, 4, 2
SECTIONS, TPS = 4, 2
PIECE = 16
FARTHEST = 8


def ctx_move(block, target):
    route = []
    for z in range(Z):
        for y in range(Y):
            for core in range(CORES):
                z2, y2, core2 = target(z, y, core)
                route.append(
                    (z * 8 + y * 2 + core, (z2 % Z) * 8 + (y2 % Y) * 2 + core2 % CORES)
                )
    return lax.ppermute(block, "ctx", route)


def copies_for_chips(block):
    return jnp.broadcast_to(block, (Z * Y,) + block.shape)


def across_chips(copies):
    groups = [[chip * CORES + core for chip in range(Z * Y)] for core in range(CORES)]
    return lax.all_to_all(copies, "ctx", 0, 0, axis_index_groups=groups)


def across_row(blocks):
    row = Y * CORES
    groups = [[z * row + place for place in range(row)] for z in range(Z)]
    return lax.all_to_all(blocks, "ctx", 0, 0, axis_index_groups=groups)


def other_core(block):
    return ctx_move(block, lambda z, y, core: (z, y, core + 1))


def passed_along(block, distance):
    count = Z * Y * CORES
    route = [(i - distance, i) for i in range(count) if 0 <= i - distance < count]
    return lax.ppermute(block, "ctx", route)


def along_section(block, step):
    return lax.ppermute(block, "section", [(s, (s + step) % SECTIONS) for s in range(SECTIONS)])


def to_other_tp(block):
    return lax.ppermute(block, "tp", [(0, 1), (1, 0)])


def section_parts(gathered, weight, section):
    mine = gathered.reshape(-1, gathered.shape[2])
    parts = []
    for rows in (mine, other_core(mine)):
        part = jnp.dot(rows, weight, preferred_element_type=jnp.float32)
        parts.append(part.reshape(SECTIONS, TPS, Y, gathered.shape[1], weight.shape[1]))

    def rows_for(step):
        place = lax.rem(section + step, SECTIONS)
        return jnp.stack(
            [lax.dynamic_index_in_dim(part, place, 0, keepdims=False) for part in parts]
        )

    return [rows_for(0)] + [rows_for(step).astype(jnp.bfloat16) for step in (1, 2, 3)]


def section_arrivals(parts):
    return [along_section(parts[step], step) for step in (3, 1, 2)]


def section_sums(own, arrivals):
    return functools.reduce(lambda total, part: total + part.astype(jnp.float32), arrivals, own)


def tp_halves(total, tp):
    keep = lax.dynamic_index_in_dim(total, tp, 1, keepdims=False)
    give = lax.dynamic_index_in_dim(total, 1 - tp, 1, keepdims=False)
    return keep, give.astype(jnp.bfloat16)


def tp_sums(keep, give):
    return keep + to_other_tp(give).astype(jnp.float32)


def row_stats(logits, columns, ids):
    picked = jnp.sum(jnp.where(columns == ids[..., None], logits, 0.0), axis=-1)
    row_top = jnp.max(logits, axis=-1)
    row_total = jnp.sum(jnp.exp(logits - row_top[..., None]), axis=-1)
    return jnp.stack([row_top, row_total, picked])


def cores_exchanged(array, axis, core):
    return jnp.where(core == 1, jnp.flip(array, axis), array)


def packed_window(keys, values, segment_ids):
    id_row = jnp.concatenate([segment_ids, jnp.zeros_like(segment_ids)])[None, :]
    return jnp.concatenate(
        [
            jnp.concatenate([keys, values], axis=1),
            jnp.broadcast_to(id_row.astype(jnp.bfloat16), (16, 2 * keys.shape[1])),
        ],
        axis=0,
    )[None]


def body(
    teacher_hidden,
    lm_head,
    sampled_ids,
    student_logprob,
    owner_map,
    queries,
    keys,
    values,
    grad_out,
    segment_ids,
):
    ctx_index = lax.axis_index("ctx")
    section = lax.axis_index("section")
    tp = lax.axis_index("tp")
    place, core = lax.rem(ctx_index, Y * CORES), lax.rem(ctx_index, CORES)

    half = teacher_hidden.shape[0] // 2
    first = across_chips(copies_for_chips(teacher_hidden[:half]))
    own_window = packed_window(keys, values, segment_ids)
    eighth = passed_along(own_window, 8)
    two_windows = jnp.concatenate([passed_along(own_window, 1), own_window], axis=0)
    first, teacher_hidden, eighth, two_windows = lax.optimization_barrier(
        (first, teacher_hidden, eighth, two_windows)
    )
    last = across_chips(copies_for_chips(teacher_hidden[half:]))
    first = section_parts(first, lm_head, section)
    arrivals = section_arrivals(first)
    arrivals[0], two_windows = lax.optimization_barrier((arrivals[0], two_windows))
    four_windows = jnp.concatenate([passed_along(two_windows, 2), two_windows], axis=0)
    first, last, four_windows = lax.optimization_barrier(
        (section_sums(first[0], arrivals), last, four_windows)
    )
    keep, give = tp_halves(first, tp)
    last = section_parts(last, lm_head, section)
    give, last = lax.optimization_barrier((give, last))
    first = tp_sums(keep, give)
    last, four_windows = lax.optimization_barrier(
        (section_sums(last[0], section_arrivals(last)), four_windows)
    )
    last = tp_sums(*tp_halves(last, tp))
    window = jnp.concatenate([eighth, passed_along(four_windows, 4), four_windows], axis=0)

    def kept_rows(array):
        rows = array.reshape(SECTIONS * TPS, Y, CORES, 2, half)
        return lax.dynamic_index_in_dim(
            rows, section * TPS + tp, 0, keepdims=False
        ).transpose(1, 0, 2, 3)

    logits = jnp.stack([first, last], axis=2)
    columns = ctx_index * lm_head.shape[1] + jnp.arange(lm_head.shape[1], dtype=jnp.int32)
    stats = row_stats(logits, columns, cores_exchanged(kept_rows(sampled_ids), 0, core))
    stats = cores_exchanged(stats, 1, core).reshape(3, -1)
    everywhere = lax.all_to_all(
        jnp.broadcast_to(stats, (Z * Y * CORES,) + stats.shape), "ctx", 0, 0
    )
    highest = jnp.max(everywhere[:, 0], axis=0)
    summed = jnp.sum(everywhere[:, 1] * jnp.exp(everywhere[:, 0] - highest), axis=0)
    teacher_logprob = jnp.sum(everywhere[:, 2], axis=0) - highest - jnp.log(summed)
    student_rows = kept_rows(student_logprob).reshape(-1)
    advantage = jnp.clip(teacher_logprob - student_rows, -clip_bound, clip_bound)
    count = SECTIONS * TPS
    everything = lax.all_to_all(
        jnp.broadcast_to(advantage, (count,) + advantage.shape), ("section", "tp"), 0, 0
    )
    owners = owner_map.reshape(SECTIONS * TPS, Y, CORES, PIECE).transpose(0, 2, 1, 3).reshape(-1)
    advantage_own = advantage.reshape(CORES, Y, PIECE).transpose(1, 0, 2).reshape(-1)
    everything = everything.reshape(-1)

    seq_rows = queries.shape[0]
    head_dim = keys.shape[1]
    group = queries.shape[1] // head_dim
    scaling = head_dim ** (-0.5)
    query_position = ctx_index * seq_rows + jnp.arange(seq_rows, dtype=jnp.int32)
    routed = jnp.sum(
        jnp.where(owners[None, :] == query_position[:, None], everything[None, :], 0.0), axis=1
    )
    weight = 1.0 + advantage_scale * routed

    key_window = window[:, :seq_rows, :head_dim].reshape(-1, head_dim)
    value_window = window[:, :seq_rows, head_dim:].reshape(-1, head_dim)
    key_segment = window[:, seq_rows, :seq_rows].reshape(-1)
    key_position = (ctx_index - FARTHEST) * seq_rows + jnp.arange(
        (FARTHEST + 1) * seq_rows, dtype=jnp.int32
    )
    allowed = (
        (key_segment[None, :] == segment_ids.astype(jnp.bfloat16)[:, None])
        & (key_position[None, :] <= query_position[:, None])
        & (key_position[None, :] >= 0)
    )
    allowed = jnp.tile(allowed, (group, 1))

    def by_head(array):
        return (
            array.reshape(seq_rows, group, head_dim)
            .transpose(1, 0, 2)
            .reshape(group * seq_rows, head_dim)
        )

    query_rows, grad_rows = by_head(queries), by_head(grad_out)
    scores = jnp.dot(query_rows, key_window.T, preferred_element_type=jnp.float32) * scaling
    masked = jnp.where(allowed, scores, masked_value)
    top = jnp.max(masked, axis=1, keepdims=True)
    raised = jnp.where(allowed, jnp.exp(masked - top), 0.0)
    softmax = (raised / jnp.sum(raised, axis=1, keepdims=True)).astype(jnp.bfloat16)
    context = jnp.dot(softmax, value_window, preferred_element_type=jnp.float32)
    row_delta = jnp.sum(grad_rows.astype(jnp.float32) * context, axis=1, keepdims=True)
    grad_prob = jnp.dot(grad_rows, value_window.T, preferred_element_type=jnp.float32)
    grad_score = (softmax.astype(jnp.float32) * (grad_prob - row_delta) * scaling).astype(
        jnp.bfloat16
    )
    grad_query = jnp.dot(grad_score, key_window, preferred_element_type=jnp.float32)

    row_weight = jnp.tile(weight, (group,))[:, None]
    grad_query = (row_weight * grad_query).astype(jnp.bfloat16)
    weighted_query = (row_weight * query_rows.astype(jnp.float32)).astype(jnp.bfloat16)
    weighted_grad = (row_weight * grad_rows.astype(jnp.float32)).astype(jnp.bfloat16)
    grad_key = jnp.dot(grad_score.T, weighted_query, preferred_element_type=jnp.float32)
    grad_value = jnp.dot(softmax.T, weighted_grad, preferred_element_type=jnp.float32)
    both = jnp.concatenate([grad_key, grad_value], axis=1).reshape(
        FARTHEST + 1, seq_rows, 2 * head_dim
    )
    d_queries = (
        grad_query.reshape(group, seq_rows, head_dim)
        .transpose(1, 0, 2)
        .reshape(seq_rows, group * head_dim)
    )
    cyclic = both[1:].astype(jnp.bfloat16)
    cyclic = jnp.concatenate([cyclic, cyclic], axis=0)
    given = lax.dynamic_slice_in_dim(cyclic, Y * CORES - 1 - place, Y * CORES, 0)
    arrived, d_queries = lax.optimization_barrier((across_row(given), d_queries))
    arrived = arrived.astype(jnp.float32)
    sender = jnp.arange(Y * CORES, dtype=jnp.int32)[:, None, None]
    back = both[0] + jnp.sum(jnp.where(sender < place, arrived, 0.0), axis=0)
    back = passed_along(back.astype(jnp.bfloat16), -Y * CORES).astype(jnp.float32)
    here = both[FARTHEST] + jnp.sum(jnp.where(sender > place, arrived, 0.0), axis=0)
    d_keys = (here[:, :head_dim] + back[:, :head_dim]).astype(jnp.bfloat16)
    d_values = (here[:, head_dim:] + back[:, head_dim:]).astype(jnp.bfloat16)
    return (advantage_own, d_queries, d_keys, d_values)


def solution(mesh):
    in_specs = (
        P("ctx", ("section", "tp")),
        P(("section", "tp"), "ctx"),
        P(),
        P(),
        P(),
        P("ctx", ("section", "tp")),
        P("ctx", ("section", "tp")),
        P("ctx", ("section", "tp")),
        P("ctx", ("section", "tp")),
        P("ctx"),
    )
    out_specs = (
        P(("section", "tp")),
        P("ctx", ("section", "tp")),
        P("ctx", ("section", "tp")),
        P("ctx", ("section", "tp")),
    )
    return jax.shard_map(body, mesh=mesh, in_specs=in_specs, out_specs=out_specs, check_vma=False)
```
